768 devices in a mesh: blk: 96 (over y_hi, z, core), rep: 8 (over y_lo, x).
Axes of the slice: x: 4, y: 8 (y_hi: 4, y_lo: 2; y = y_hi * 2 + y_lo), z: 12, core: 2. Of those that a mesh axis runs over, the one named last changes fastest.
Arguments:
- feats: bfloat16 [196608, 128], P(('blk', 'rep')), may hold values from -6 to 6
- tiles: bfloat16 [1536, 48, 128, 128], P(('blk', 'rep')), may hold values from -0.078125 to 0.078125
- cols: int32 [1536, 48], P(('blk', 'rep')), may hold values from 0 to 1535, as said below
- counts: int32 [1536], P(('blk', 'rep')), may hold values from 2 to 48, as said below
- w_self: bfloat16 [128, 256], replicated, may hold values from -0.5 to 0.5
- w_neigh: bfloat16 [128, 256], replicated, may hold values from -0.5 to 0.5
- bias: float32 [256], replicated, may hold values from -3 to 3
- cotangent: bfloat16 [196608, 256], P(('blk', 'rep')), may hold values from -6 to 6
Outputs:
- hidden: bfloat16 [196608, 256], P(('blk', 'rep'))
- grad_feats: bfloat16 [196608, 128], P(('blk', 'rep'))
- grad_self: float32 [128, 256], replicated
- grad_neigh: float32 [128, 256], replicated
- grad_bias: float32 [256], replicated
The draws below stay inside these ranges and needn't reach their ends.
Inputs may be any that keep to these rules, and one draw needn't show every extreme that they name: `cols`: let g(b) = b // 16. The column blocks of row block b lie among the blocks of groups g(b) - 1 to g(b) + 1, counted modulo 96, where group g holds blocks g * 16 to (g + 1) * 16 - 1; the first row block of every group names the first block of group g(b) - 1 and the last block of group g(b) + 1. Slots k >= counts[b] are unused; the first row block of every group of 16 uses all 48 slots.
All inputs are finite; a program needn't handle non-finite values.
Results may differ from the reference program's by a relative error of at most 0.0075.
Values may be sent and summed in bfloat16 or wider, within the bound.
No kernel may reach another device: no remote copies, remote signals or barrier semaphores. Data moves between devices by JAX's collectives and lax.ppermute only.
A program may use at most 32 MiB of HBM per device.

```python
import math
import jax
import jax.numpy as jnp
from jax import lax

F = 128
HID = 256
BS = 128
K = 48
REACH = 1
NB_DEV = 16
NBLOCKS = 1536
NODES = 196608


def draw_cols(key, part):
    key = jax.random.fold_in(key, 11)
    span = (2 * REACH + 1) * NB_DEV
    offsets = jax.random.randint(key, (NBLOCKS, K), 0, span)
    rows = jnp.arange(NBLOCKS)
    first = rows % NB_DEV == 0
    offsets = offsets.at[:, 0].set(jnp.where(first, 0, offsets[:, 0]))
    offsets = offsets.at[:, 1].set(jnp.where(first, span - 1, offsets[:, 1]))
    owner = rows // NB_DEV
    base = (owner - REACH) * NB_DEV
    return ((base[:, None] + offsets + NBLOCKS) % NBLOCKS).astype(jnp.int32)


def draw_counts(key, part):
    key = jax.random.fold_in(key, 23)
    first_key, second_key = jax.random.split(key)
    one = jax.random.randint(first_key, (NBLOCKS,), 2, K + 1)
    two = jax.random.randint(second_key, (NBLOCKS,), 2, K + 1)
    drawn = jnp.minimum(one, two)
    first = jnp.arange(NBLOCKS) % NB_DEV == 0
    return jnp.where(first, K, drawn).astype(jnp.int32)


def block_levels(rng, dims, shards, least, largest):
    gain, own = 1.0, jax.random.fold_in(rng, 6)
    for dim, shards_of in shards:
        steps = jnp.exp(jax.random.uniform(jax.random.fold_in(own, dim), (shards_of,), jnp.float32, least / len(shards), largest / len(shards)))
        gain = gain * jnp.repeat(steps, dims[dim] // shards_of).reshape([-1 if axis == dim else 1 for axis in range(len(dims))])
    return gain


def noise(own_key, extent, width, most, cuts=(), kind=jnp.bfloat16):
    entries = jax.random.normal(own_key, extent, jnp.float32) * width
    if len(cuts) > 0:
        entries = block_levels(own_key, extent, cuts, -0.22, 0.18) * entries
    return jnp.clip(entries, min=-most, max=most).astype(kind)


def setup_inputs(seed: int = 0) -> dict:
    arg_keys = jax.random.split(jax.random.key(seed), 9)
    feats = noise(arg_keys[0], (NODES, F), 1.0, 6.0, ((0, 768),))
    tiles = noise(arg_keys[1], (NBLOCKS, K, BS, BS), (BS * K) ** -0.5, 0.078125, ((0, 768),))
    cols = draw_cols(jax.random.fold_in(arg_keys[8], 71), 0)
    counts = draw_counts(jax.random.fold_in(arg_keys[8], 71), 0)
    w_self = noise(arg_keys[4], (F, HID), F ** -0.5, 0.5)
    w_neigh = noise(arg_keys[5], (F, HID), F ** -0.5, 0.5)
    bias = noise(arg_keys[6], (HID,), 0.5, 3.0, (), jnp.float32)
    cotangent = noise(arg_keys[7], (NODES, HID), 1.0, 6.0, ((0, 768),))
    return {"feats": feats, "tiles": tiles, "cols": cols, "counts": counts, "w_self": w_self, "w_neigh": w_neigh, "bias": bias, "cotangent": cotangent}


def reference(feats, tiles, cols, counts, w_self, w_neigh, bias, cotangent):
    nblocks = cols.shape[0]
    groups = nblocks // NB_DEV
    nodes = nblocks * BS
    blocks = feats.reshape(nblocks, BS, F)
    valid = jnp.arange(K)[None, :] < counts[:, None]
    tile_groups = tiles.reshape(groups, NB_DEV, K, BS, BS)
    col_groups = cols.reshape(groups, NB_DEV, K)
    valid_groups = valid.reshape(groups, NB_DEV, K)

    def aggregate(inputs):
        tile, col, used = inputs
        picked = blocks[col].astype(jnp.float32)
        masked = jnp.where(used[:, :, None, None], tile.astype(jnp.float32), 0.0)
        return jnp.einsum('bkij,bkjf->bif', masked, picked)
    agg = lax.map(aggregate, (tile_groups, col_groups, valid_groups)).reshape(nodes, F).astype(jnp.bfloat16)
    pre = jnp.dot(feats, w_self, preferred_element_type=jnp.float32) + jnp.dot(agg, w_neigh, preferred_element_type=jnp.float32) + bias
    hidden = jax.nn.silu(pre).astype(jnp.bfloat16)
    sig = jax.nn.sigmoid(pre)
    dpre = (cotangent.astype(jnp.float32) * sig * (1.0 + pre * (1.0 - sig))).astype(jnp.bfloat16)
    factor = 1.0 / math.sqrt(nodes)
    grad_self = jnp.dot(feats.T, dpre, preferred_element_type=jnp.float32) * factor
    grad_neigh = jnp.dot(agg.T, dpre, preferred_element_type=jnp.float32) * factor
    grad_bias = lax.optimization_barrier(jnp.sum(dpre.astype(jnp.float32), axis=0)) * factor
    back = jnp.dot(dpre, w_neigh.T, preferred_element_type=jnp.float32).astype(jnp.bfloat16)
    back_groups = back.reshape(groups, NB_DEV, BS, F)

    def scatter_back(carry, inputs):
        tile, col, used, rows = inputs
        masked = jnp.where(used[:, :, None, None], tile.astype(jnp.float32), 0.0)
        terms = jnp.einsum('bkij,bif->bkjf', masked, rows.astype(jnp.float32))
        carry = carry.at[col.reshape(-1)].add(terms.reshape(-1, BS, F))
        return (carry, None)
    start_sum = jnp.zeros((nblocks, BS, F), jnp.float32)
    returned, unused = lax.scan(scatter_back, start_sum, (tile_groups, col_groups, valid_groups, back_groups))
    own = jnp.dot(dpre, w_self.T, preferred_element_type=jnp.float32)
    grad_feats = (own + returned.reshape(nodes, F)).astype(jnp.bfloat16)
    return (hidden, grad_feats, grad_self, grad_neigh, grad_bias)
```

```python
import functools
import math

import jax
import jax.numpy as jnp
from jax import lax
from jax.experimental import pallas as pl
from jax.experimental.pallas import tpu as pltpu
from jax.sharding import Mesh, PartitionSpec as P

BS = 128
K = 48
F = 128
HID = 256
GROUP = 16
BLOCKS_DEV = 2
SPAN = 3
REPS = 8
ROWS = BLOCKS_DEV * BS
CHUNK = 8
REP = ("yl", "x")
BLK = ("yh", "z", "core")
EVERY = BLK + REP
YH = 4
PART = 24
GRAD_ROWS = YH * PART
TERM_ROWS = SPAN * ROWS
bf16 = jnp.bfloat16
f32 = jnp.float32


def layer_kernel(
    pos_ref, cols_ref, counts_ref, feats_ref, wself_ref, wneigh_ref, bias_ref, cot_ref,
    tiles_hbm, window_hbm,
    hidden_ref, own_ref, send_ref,
    tiles, window, total, dense, tile_sem, window_sem,
):
    chunks = BLOCKS_DEV * K // CHUNK
    per_block = K // CHUNK

    def tile_copy(c):
        b, k = c // per_block, (c % per_block) * CHUNK
        part = (b, pl.ds(k, CHUNK))
        return pltpu.make_async_copy(tiles_hbm.at[part], tiles.at[part], tile_sem.at[c])

    blocks = REPS * SPAN * BLOCKS_DEV
    window_copy = pltpu.make_async_copy(window_hbm, window.at[pl.ds(0, blocks)], window_sem)
    window_copy.start()
    for c in range(chunks):
        tile_copy(c).start()
    window[blocks] = jnp.zeros((BS, F), bf16)
    for i in range(blocks):
        total[i] = jnp.zeros((F, BS), f32)

    nblocks = pos_ref[1]
    base = (pos_ref[0] - 1) * GROUP

    def place(b, k):
        d = cols_ref[b, k] - base
        d = jnp.where(d < 0, d + nblocks, d)
        d = jnp.where(d >= nblocks, d - nblocks, d)
        member = lax.shift_right_logical(jnp.bitwise_and(d, GROUP - 1), 1)
        at = member * (SPAN * BLOCKS_DEV) + lax.shift_right_logical(d, 4) * BLOCKS_DEV + jnp.bitwise_and(d, 1)
        return jnp.where(k < counts_ref[b], at, blocks)

    window_copy.wait()
    for b in range(BLOCKS_DEV):
        acc = jnp.zeros((BS, F), f32)
        for c in range(per_block):
            tile_copy(b * per_block + c).wait()
            for k in range(c * CHUNK, (c + 1) * CHUNK, 2):
                lhs = jnp.concatenate([tiles[b, k], tiles[b, k + 1]], axis=1)
                rhs = jnp.concatenate([window[place(b, k)], window[place(b, k + 1)]], axis=0)
                acc = acc + jnp.dot(lhs, rhs, preferred_element_type=f32)
        dense[pl.ds(b * BS, BS), F:] = acc.astype(bf16)
    dense[:, :F] = feats_ref[...]
    both = dense[...]
    weights = jnp.concatenate([wself_ref[...], wneigh_ref[...]], axis=0)
    pre = jnp.dot(both, weights, preferred_element_type=f32) + bias_ref[...]
    sig = jax.nn.sigmoid(pre)
    hidden_ref[...] = (pre * sig).astype(bf16)
    dpre = (cot_ref[...].astype(f32) * (sig * (1.0 + pre * (1.0 - sig)))).astype(bf16)
    contract_cols = (((1,), (1,)), ((), ()))
    contract_rows = (((0,), (0,)), ((), ()))
    own_ref[...] = lax.dot_general(dpre, wself_ref[...], contract_cols, preferred_element_type=f32)
    back = lax.dot_general(wneigh_ref[...], dpre, contract_cols, preferred_element_type=f32).astype(bf16)
    grads = lax.dot_general(both, dpre, contract_rows, preferred_element_type=f32)
    bias_sum = jnp.sum(dpre.astype(f32), axis=0, keepdims=True)

    for b in range(BLOCKS_DEV):
        back_b = back[:, b * BS:(b + 1) * BS]
        for k in range(0, K, 2):
            rhs = jnp.concatenate([tiles[b, k], tiles[b, k + 1]], axis=1)
            terms = jnp.dot(back_b, rhs, preferred_element_type=f32)
            one, two = place(b, k), place(b, k + 1)
            total[one] = total[one] + terms[:, :BS]
            total[two] = total[two] + terms[:, BS:]

    for r in range(REPS):
        for i in range(SPAN * BLOCKS_DEV):
            send_ref[r, pl.ds(i * BS, BS)] = total[r * SPAN * BLOCKS_DEV + i].astype(bf16)
    wide = HID // BS
    for r in range(REPS):
        for y in range(YH):
            p = r * YH + y
            rows = []
            for h in range(wide):
                rows.append(grads[p * 8:(p + 1) * 8, h * BS:(h + 1) * BS])
            h = p // (REPS * YH // wide)
            rows.append(jnp.broadcast_to(bias_sum[:, h * BS:(h + 1) * BS], (8, BS)))
            value = jnp.concatenate(rows, axis=0)
            high = value.astype(bf16)
            low = (value - high.astype(f32)).astype(bf16)
            at = TERM_ROWS + y * 2 * PART
            send_ref[r, pl.ds(at, 2 * PART)] = jnp.concatenate([high, low], axis=0)


def local_layer(pos, cols, counts, feats, w_self, w_neigh, bias, cotangent, tiles, window):
    smem = pl.BlockSpec(memory_space=pltpu.SMEM)
    vmem = pl.BlockSpec(memory_space=pltpu.VMEM)
    anywhere = pl.BlockSpec(memory_space=pl.ANY)
    blocks = REPS * SPAN * BLOCKS_DEV
    return pl.pallas_call(
        layer_kernel,
        out_shape=(
            jax.ShapeDtypeStruct((ROWS, HID), bf16),
            jax.ShapeDtypeStruct((ROWS, F), f32),
            jax.ShapeDtypeStruct((REPS, TERM_ROWS + 2 * GRAD_ROWS, BS), bf16),
        ),
        in_specs=[smem] * 3 + [vmem] * 5 + [anywhere] * 2,
        out_specs=(vmem, vmem, vmem),
        scratch_shapes=[
            pltpu.VMEM((BLOCKS_DEV, K, BS, BS), bf16),
            pltpu.VMEM((blocks + 1, BS, F), bf16),
            pltpu.VMEM((blocks + 1, F, BS), f32),
            pltpu.VMEM((ROWS, 2 * F), bf16),
            pltpu.SemaphoreType.DMA((BLOCKS_DEV * K // CHUNK,)),
            pltpu.SemaphoreType.DMA,
        ],
        compiler_params=pltpu.CompilerParams(vmem_limit_bytes=32 * 2**20),
        name="local_layer",
    )(pos, cols, counts, feats, w_self, w_neigh, bias, cotangent, tiles, window)


def sum_kernel(got_ref, mine_ref, near_ref, grad_ref):
    for i in range(SPAN * BLOCKS_DEV):
        rows = pl.ds(i * BS, BS)
        acc = got_ref[0, rows].astype(f32)
        for r in range(1, REPS):
            acc = acc + got_ref[r, rows].astype(f32)
        o, j = i // BLOCKS_DEV, i % BLOCKS_DEV
        if o == 1:
            mine_ref[j] = acc
        else:
            near_ref[o // 2, pl.ds(j * BS, BS)] = acc.astype(bf16)
    for y in range(YH):
        both = pl.ds(TERM_ROWS + y * 2 * PART, 2 * PART)
        acc = got_ref[0, both].astype(f32)
        for r in range(1, REPS):
            acc = acc + got_ref[r, both].astype(f32)
        grad_ref[y] = acc[:PART] + acc[PART:]


def sum_terms(got):
    vmem = pl.BlockSpec(memory_space=pltpu.VMEM)
    return pl.pallas_call(
        sum_kernel,
        out_shape=(
            jax.ShapeDtypeStruct((BLOCKS_DEV, F, BS), f32),
            jax.ShapeDtypeStruct((2, ROWS, BS), bf16),
            jax.ShapeDtypeStruct((YH, PART, BS), f32),
        ),
        in_specs=[vmem],
        out_specs=(vmem, vmem, vmem),
        compiler_params=pltpu.CompilerParams(vmem_limit_bytes=32 * 2**20),
        name="sum_terms",
    )(got)


def final_kernel(own_ref, mine_ref, near_ref, far_ref, out_ref):
    for j in range(BLOCKS_DEV):
        rows = pl.ds(j * BS, BS)
        terms = mine_ref[j] + near_ref[rows].astype(f32) + far_ref[rows].astype(f32)
        out_ref[rows] = (own_ref[rows] + terms.T).astype(bf16)


def final_sum(own, mine, near, far):
    vmem = pl.BlockSpec(memory_space=pltpu.VMEM)
    return pl.pallas_call(
        final_kernel,
        out_shape=jax.ShapeDtypeStruct((ROWS, F), bf16),
        in_specs=[vmem] * 4,
        out_specs=vmem,
        name="final_sum",
    )(own, mine, near, far)


def swapped(value, pairs):
    return lax.ppermute(value, BLK, pairs)


def broadcast_along(value, axes, count):
    return lax.all_to_all(jnp.broadcast_to(value[None], (count,) + value.shape), axes, 0, 0)


def shards(cycle, feats, tiles, cols, counts, w_self, w_neigh, bias, cotangent):
    position = lax.axis_index(BLK)
    even = (position % 2) == 0
    pos = jnp.stack([position, jnp.int32(cycle * GROUP)]).astype(jnp.int32)
    inner = [(i, i ^ 1) for i in range(cycle)]
    outer = [(i, (((i + 1) ^ 1) - 1) % cycle) for i in range(cycle)]
    across = swapped(feats, outer)
    beside = swapped(feats, inner)
    before = jnp.where(even, across, beside)
    after = jnp.where(even, beside, across)
    mine = jnp.concatenate([before, feats, after], axis=0)
    window = broadcast_along(mine, REP, REPS)
    window = window.reshape(REPS * SPAN * BLOCKS_DEV, BS, F)
    hidden, own, send = local_layer(
        pos, cols, counts, feats, w_self, w_neigh, bias.reshape(1, HID), cotangent, tiles, window
    )
    got = lax.all_to_all(send, REP, 0, 0)
    terms, near, grad = sum_terms(got)
    to_across = jnp.where(even, near[0], near[1])
    to_beside = jnp.where(even, near[1], near[0])
    from_across = swapped(to_across, outer)
    from_beside = swapped(to_beside, inner)
    grad_feats = final_sum(own, terms, from_across, from_beside)
    grad = jnp.sum(lax.all_to_all(grad, "yh", 0, 0), axis=0)
    grad = jnp.sum(broadcast_along(grad, ("z", "core"), cycle // YH), axis=0)
    factor = 1.0 / math.sqrt(cycle * REPS * ROWS)
    parts = broadcast_along(grad * factor, ("yh",) + REP, YH * REPS)
    parts = parts.reshape(YH, REPS, PART, BS).transpose(1, 0, 2, 3).reshape(REPS * YH, PART, BS)
    wide = HID // BS
    weights = parts[:, :8 * wide].reshape(REPS * YH, wide, 8, BS)
    weights = weights.transpose(0, 2, 1, 3).reshape(2, F, HID)
    grad_bias = jnp.concatenate([parts[0, 8 * wide], parts[REPS * YH // wide, 8 * wide]])
    return (hidden, grad_feats, weights[0], weights[1], grad_bias)


def solution(mesh):
    cycle, reps = mesh.shape["blk"], mesh.shape["rep"]
    split = Mesh(
        mesh.devices.reshape(YH, cycle // YH // 2, 2, 2, reps // 2), EVERY
    )
    in_specs = (
        P(EVERY, None),
        P(EVERY, None, None, None),
        P(EVERY, None),
        P(EVERY),
        P(),
        P(),
        P(),
        P(EVERY, None),
    )
    out_specs = (P(EVERY, None), P(EVERY, None), P(), P(), P())
    return jax.shard_map(
        functools.partial(shards, cycle),
        mesh=split, in_specs=in_specs, out_specs=out_specs, check_vma=False,
    )
```

```python
import functools
import math

import jax
import jax.numpy as jnp
from jax import lax
from jax.experimental import pallas as pl
from jax.experimental.pallas import tpu as pltpu
from jax.sharding import Mesh, PartitionSpec as P

BS = 128
K = 48
F = 128
HID = 256
GROUP = 16
BLOCKS_DEV = 2
SPAN = 3
REPS = 8
ROWS = BLOCKS_DEV * BS
WINDOW = SPAN * GROUP
REP = ("yl", "x")
BLK = ("yh", "z", "core")
EVERY = BLK + REP
YH = 4
ALONG_X = 4
PIECE = 2 * BLOCKS_DEV
PARTS = YH * REPS
PART = 24
WIDE = HID // BS
BIAS_AT = 8 * WIDE
bf16 = jnp.bfloat16
f32 = jnp.float32
SMEM = pl.BlockSpec(memory_space=pltpu.SMEM)
VMEM = pl.BlockSpec(memory_space=pltpu.VMEM)
CONTRACT_COLS = (((1,), (1,)), ((), ()))
CONTRACT_ROWS = (((0,), (0,)), ((), ()))


def params(mib):
    return pltpu.CompilerParams(vmem_limit_bytes=mib * 2**20)


def cost(flops, bytes_accessed):
    return pl.CostEstimate(flops=flops, bytes_accessed=bytes_accessed, transcendentals=0)


def window_places(cols, counts, position, cycle):
    blocks = cycle * GROUP
    places = (cols - (position - 1) * GROUP + blocks) % blocks
    used = jnp.arange(K, dtype=jnp.int32)[None, :] < counts[:, None]
    return jnp.where(used, places, WINDOW)


def layer_kernel(
    pos_ref, place_ref, weights, bias_ref, cot,
    tiles_ref, mine_ref, beside_ref, across_ref,
    hidden_ref, grad_ref, kept_ref, away_ref,
    window, dense, total,
):
    even = jnp.bitwise_and(pos_ref[0], 1) == 0
    beside_at = jnp.where(even, 2 * GROUP, 0)
    across_at = jnp.where(even, 0, 2 * GROUP)
    window[WINDOW] = jnp.zeros((BS, F), bf16)
    for i in range(GROUP):
        r, rows = i // BLOCKS_DEV, pl.ds((i % BLOCKS_DEV) * BS, BS)
        window[GROUP + i] = mine_ref[r, rows]
        window[beside_at + i] = beside_ref[r, rows]
        window[across_at + i] = across_ref[r, rows]
    for i in range(WINDOW):
        total[i] = jnp.zeros((F, BS), f32)
    for b in range(BLOCKS_DEV):
        acc = jnp.zeros((BS, F), f32)
        for k in range(0, K, 2):
            lhs = jnp.concatenate([tiles_ref[b, k], tiles_ref[b, k + 1]], axis=1)
            rhs = jnp.concatenate([window[place_ref[b, k]], window[place_ref[b, k + 1]]], axis=0)
            acc = acc + jnp.dot(lhs, rhs, preferred_element_type=f32)
        dense[pl.ds(b * BS, BS), F:] = acc.astype(bf16)
    dense[:, :F] = mine_ref[pos_ref[1]]
    both = dense[...]
    pre = jnp.dot(both, weights[...], preferred_element_type=f32) + bias_ref[...]
    sig = jax.nn.sigmoid(pre)
    hidden_ref[...] = (pre * sig).astype(bf16)
    dpre = (cot[...].astype(f32) * (sig * (1.0 + pre * (1.0 - sig)))).astype(bf16)
    backs = lax.dot_general(weights[...], dpre, CONTRACT_COLS, preferred_element_type=f32)
    grads = lax.dot_general(both, dpre, CONTRACT_ROWS, preferred_element_type=f32)
    bias_sum = jnp.sum(dpre.astype(f32), axis=0, keepdims=True)
    for p in range(PARTS):
        rows = [grads[p * 8:(p + 1) * 8, h * BS:(h + 1) * BS] for h in range(WIDE)]
        h = p // (PARTS // WIDE)
        rows.append(jnp.broadcast_to(bias_sum[:, h * BS:(h + 1) * BS], (8, BS)))
        grad_ref[p] = jnp.concatenate(rows, axis=0).astype(bf16)

    for b in range(BLOCKS_DEV):
        back = backs[F:, b * BS:(b + 1) * BS].astype(bf16)
        for k in range(0, K, 2):
            rhs = jnp.concatenate([tiles_ref[b, k], tiles_ref[b, k + 1]], axis=1)
            terms = jnp.dot(back, rhs, preferred_element_type=f32)
            one, two = place_ref[b, k], place_ref[b, k + 1]
            total[one] = total[one] + terms[:, :BS]
            total[two] = total[two] + terms[:, BS:]
    for j in range(BLOCKS_DEV):
        own = GROUP + BLOCKS_DEV * pos_ref[1] + j
        total[own] = total[own] + backs[:F, j * BS:(j + 1) * BS]
    for i in range(GROUP):
        away_ref[i] = total[beside_at + i].astype(bf16)
        kept_ref[0, i] = total[GROUP + i].astype(bf16)
        kept_ref[1, i] = total[across_at + i].astype(bf16)


def local_layer(pos, places, weights, bias, cotangent, tiles, mine, beside, across):
    return pl.pallas_call(
        layer_kernel,
        out_shape=(
            jax.ShapeDtypeStruct((ROWS, HID), bf16),
            jax.ShapeDtypeStruct((PARTS, PART, BS), bf16),
            jax.ShapeDtypeStruct((2, GROUP, F, BS), bf16),
            jax.ShapeDtypeStruct((GROUP, F, BS), bf16),
        ),
        in_specs=[SMEM] * 2 + [VMEM] * 7,
        out_specs=(VMEM,) * 4,
        scratch_shapes=[
            pltpu.VMEM((WINDOW + 1, BS, F), bf16),
            pltpu.VMEM((ROWS, 2 * F), bf16),
            pltpu.VMEM((WINDOW + 1, F, BS), f32),
        ],
        compiler_params=params(28),
        cost_estimate=cost(4 * BLOCKS_DEV * K * BS**3, 8 * 2**20),
        name="local_layer",
    )(pos, places, weights, bias, cotangent, tiles, mine, beside, across)


def chunk_kernel(pos_ref, kept_ref, beside_ref, stay_ref, send_ref):
    for dy, out_ref in enumerate((stay_ref, send_ref)):
        for dx in range(ALONG_X):
            first = jnp.bitwise_xor(pos_ref[1], dy * ALONG_X + dx) * BLOCKS_DEV
            for j in range(BLOCKS_DEV):
                own = kept_ref[0, first + j].astype(f32) + beside_ref[first + j].astype(f32)
                out_ref[dx * PIECE + j] = own.astype(bf16)
                out_ref[dx * PIECE + BLOCKS_DEV + j] = kept_ref[1, first + j]


def chunks_of(pos, kept, beside):
    return pl.pallas_call(
        chunk_kernel,
        out_shape=(jax.ShapeDtypeStruct((GROUP, F, BS), bf16),) * 2,
        in_specs=[SMEM] + [VMEM] * 2,
        out_specs=(VMEM,) * 2,
        compiler_params=params(8),
        cost_estimate=cost(GROUP * F * BS, 3 * 2**20),
        name="chunks",
    )(pos, kept, beside)


def sum_y_kernel(stay_ref, got_ref, here_ref, *send_refs):
    for i in range(PIECE):
        here_ref[i] = stay_ref[i].astype(f32) + got_ref[i].astype(f32)
    for d, send_ref in enumerate(send_refs):
        for i in range(PIECE):
            at = (d + 1) * PIECE + i
            send_ref[i] = (stay_ref[at].astype(f32) + got_ref[at].astype(f32)).astype(bf16)


def sum_y(stay, got):
    piece = (PIECE, F, BS)
    return pl.pallas_call(
        sum_y_kernel,
        out_shape=(jax.ShapeDtypeStruct(piece, f32),) + (jax.ShapeDtypeStruct(piece, bf16),) * (ALONG_X - 1),
        in_specs=[VMEM] * 2,
        out_specs=(VMEM,) * ALONG_X,
        compiler_params=params(8),
        cost_estimate=cost(GROUP * F * BS, 2 * 2**20),
        name="sum_y",
    )(stay, got)


def sum_x_kernel(here_ref, *refs):
    got_refs, (own_ref, across_ref) = refs[:-2], refs[-2:]
    for i in range(PIECE):
        acc = here_ref[i]
        for got_ref in got_refs:
            acc = acc + got_ref[i].astype(f32)
        if i < BLOCKS_DEV:
            own_ref[i] = acc
        else:
            across_ref[i - BLOCKS_DEV] = acc.astype(bf16)


def sum_x(here, got):
    return pl.pallas_call(
        sum_x_kernel,
        out_shape=(
            jax.ShapeDtypeStruct((BLOCKS_DEV, F, BS), f32),
            jax.ShapeDtypeStruct((BLOCKS_DEV, F, BS), bf16),
        ),
        in_specs=[VMEM] * ALONG_X,
        out_specs=(VMEM,) * 2,
        compiler_params=params(8),
        cost_estimate=cost(PIECE * ALONG_X * F * BS, 2**20),
        name="sum_x",
    )(here, *got)


def final_kernel(own_ref, across_ref, out_ref):
    for j in range(BLOCKS_DEV):
        terms = own_ref[j] + across_ref[j].astype(f32)
        out_ref[pl.ds(j * BS, BS)] = terms.T.astype(bf16)


def final_sum(own, across):
    return pl.pallas_call(
        final_kernel,
        out_shape=jax.ShapeDtypeStruct((ROWS, F), bf16),
        in_specs=[VMEM] * 2,
        out_specs=VMEM,
        compiler_params=params(8),
        cost_estimate=cost(ROWS * F, 2**19),
        name="final_sum",
    )(own, across)


def spread_kernel(scale, count, got_ref, out_ref):
    total = got_ref[0].astype(f32)
    for i in range(1, got_ref.shape[0]):
        total = total + got_ref[i].astype(f32)
    total = (total * scale).astype(bf16)
    for i in range(count):
        out_ref[i] = total


def sum_and_spread(got, scale, count):
    return pl.pallas_call(
        functools.partial(spread_kernel, scale, count),
        out_shape=jax.ShapeDtypeStruct((count,) + got.shape[1:], bf16),
        in_specs=[VMEM],
        out_specs=VMEM,
        compiler_params=params(8),
        cost_estimate=cost(got.size, 8 * got.size),
        name="sum_and_spread",
    )(got)


def unpack_kernel(parts_ref, self_ref, neigh_ref, bias_ref):
    for p in range(PARTS):
        out_ref = self_ref if p < PARTS // 2 else neigh_ref
        rows = pl.ds((p % (PARTS // 2)) * 8, 8)
        part = parts_ref[p].astype(f32)
        for h in range(WIDE):
            out_ref[rows, pl.ds(h * BS, BS)] = part[h * 8:(h + 1) * 8]
    for h in range(WIDE):
        part = parts_ref[h * (PARTS // WIDE)].astype(f32)
        bias_ref[:, pl.ds(h * BS, BS)] = part[BIAS_AT:BIAS_AT + 1]


def unpack(parts):
    return pl.pallas_call(
        unpack_kernel,
        out_shape=(
            jax.ShapeDtypeStruct((F, HID), f32),
            jax.ShapeDtypeStruct((F, HID), f32),
            jax.ShapeDtypeStruct((1, HID), f32),
        ),
        in_specs=[VMEM],
        out_specs=(VMEM,) * 3,
        compiler_params=params(8),
        cost_estimate=cost(parts.size, 8 * parts.size),
        name="unpack",
    )(parts)


def swapped(value, pairs):
    return lax.ppermute(value, BLK, pairs)


def exchanged(value, axes):
    return lax.all_to_all(value, axes, 0, 0)


def gathered(value):
    return exchanged(jnp.broadcast_to(value[None], (REPS,) + value.shape), REP)


def shards(cycle, feats, tiles, cols, counts, w_self, w_neigh, bias, cotangent):
    position = lax.axis_index(BLK)
    pos = jnp.stack([position, lax.axis_index(REP)]).astype(jnp.int32)
    places = window_places(cols, counts, position, cycle)
    weights = jnp.concatenate([w_self, w_neigh], axis=0)
    inner = [(i, i ^ 1) for i in range(cycle)]
    outer = [(i, (((i + 1) ^ 1) - 1) % cycle) for i in range(cycle)]
    across_rows = swapped(feats, outer)
    mine = gathered(feats)
    across = gathered(across_rows)
    beside = swapped(mine, inner)
    hidden, grad, kept, away = local_layer(
        pos, places, weights, bias.reshape(1, HID), cotangent, tiles, mine, beside, across,
    )
    split = ("yh",) + REP
    layers = ("z", "core")
    grad = exchanged(grad, split)
    stay, to_y = chunks_of(pos, kept, swapped(away, inner))
    from_y = lax.ppermute(to_y, "yl", [(0, 1), (1, 0)])
    from_y, grad = lax.optimization_barrier((from_y, grad))
    grad = exchanged(sum_and_spread(grad, 1.0, cycle // YH), layers)
    here, *to_x = sum_y(stay, from_y)
    from_x = []
    for d in range(1, ALONG_X):
        from_x.append(lax.ppermute(to_x[d - 1], "x", [(x, x ^ d) for x in range(ALONG_X)]))
    own, to_across = sum_x(here, from_x)
    to_across, grad = lax.optimization_barrier((to_across, grad))
    factor = 1.0 / math.sqrt(cycle * REPS * ROWS)
    grad = exchanged(sum_and_spread(grad, factor, PARTS), split)
    grad_feats = final_sum(own, swapped(to_across, outer))
    grad_self, grad_neigh, grad_bias = unpack(grad)
    return (hidden, grad_feats, grad_self, grad_neigh, grad_bias.reshape(HID))


def solution(mesh):
    cycle, reps = mesh.shape["blk"], mesh.shape["rep"]
    split = Mesh(
        mesh.devices.reshape(YH, cycle // YH // 2, 2, 2, reps // 2), EVERY
    )
    in_specs = (
        P(EVERY, None),
        P(EVERY, None, None, None),
        P(EVERY, None),
        P(EVERY),
        P(),
        P(),
        P(),
        P(EVERY, None),
    )
    out_specs = (P(EVERY, None), P(EVERY, None), P(), P(), P())
    return jax.shard_map(
        functools.partial(shards, cycle),
        mesh=split, in_specs=in_specs, out_specs=out_specs, check_vma=False,
    )
```

```python
import functools
import math

import jax
import jax.numpy as jnp
from jax import lax
from jax.experimental import pallas as pl
from jax.experimental.pallas import tpu as pltpu
from jax.sharding import Mesh, PartitionSpec as P

BS = 128
K = 48
F = 128
HID = 256
GROUP = 16
BLOCKS_DEV = 2
SPAN = 3
REPS = 8
ROWS = BLOCKS_DEV * BS
WINDOW = SPAN * GROUP
REP = ("yl", "x")
BLK = ("yh", "z", "core")
EVERY = BLK + REP
YH = 4
ALONG_X = 4
PIECE = 2 * BLOCKS_DEV
PARTS = 24
PART = 24
WIDE = HID // BS
TILES = (2 * F // 8 + 1) * WIDE
bf16 = jnp.bfloat16
f32 = jnp.float32
SMEM = pl.BlockSpec(memory_space=pltpu.SMEM)
VMEM = pl.BlockSpec(memory_space=pltpu.VMEM)
CONTRACT_COLS = (((1,), (1,)), ((), ()))
CONTRACT_ROWS = (((0,), (0,)), ((), ()))


def params(mib):
    return pltpu.CompilerParams(vmem_limit_bytes=mib * 2**20)


def cost(flops, bytes_accessed):
    return pl.CostEstimate(flops=flops, bytes_accessed=bytes_accessed, transcendentals=0)


def window_places(cols, counts, position, cycle):
    blocks = cycle * GROUP
    places = (cols - (position - 1) * GROUP + blocks) % blocks
    used = jnp.arange(K, dtype=jnp.int32)[None, :] < counts[:, None]
    return jnp.where(used, places, WINDOW)


def index_along(axes):
    index = 0
    for axis in axes:
        index = index * lax.axis_size(axis) + lax.axis_index(axis)
    return index


def layer_kernel(
    pos_ref, place_ref, weights, bias_ref, cot,
    tiles_ref, mine_ref, beside_ref, across_ref,
    hidden_ref, grad_ref, kept_ref, away_ref,
    window, dense, total,
):
    even = jnp.bitwise_and(pos_ref[0], 1) == 0
    beside_at = jnp.where(even, 2 * GROUP, 0)
    across_at = jnp.where(even, 0, 2 * GROUP)
    window[WINDOW] = jnp.zeros((BS, F), bf16)
    for i in range(GROUP):
        r, rows = i // BLOCKS_DEV, pl.ds((i % BLOCKS_DEV) * BS, BS)
        window[GROUP + i] = mine_ref[r, rows]
        window[beside_at + i] = beside_ref[r, rows]
        window[across_at + i] = across_ref[r, rows]
    for i in range(WINDOW):
        total[i] = jnp.zeros((F, BS), f32)
    for b in range(BLOCKS_DEV):
        acc = jnp.zeros((BS, F), f32)
        for k in range(0, K, 2):
            lhs = jnp.concatenate([tiles_ref[b, k], tiles_ref[b, k + 1]], axis=1)
            rhs = jnp.concatenate([window[place_ref[b, k]], window[place_ref[b, k + 1]]], axis=0)
            acc = acc + jnp.dot(lhs, rhs, preferred_element_type=f32)
        dense[pl.ds(b * BS, BS), F:] = acc.astype(bf16)
    dense[:, :F] = mine_ref[pos_ref[1]]
    both = dense[...]
    pre = jnp.dot(both, weights[...], preferred_element_type=f32) + bias_ref[...]
    sig = jax.nn.sigmoid(pre)
    hidden_ref[...] = (pre * sig).astype(bf16)
    dpre = (cot[...].astype(f32) * (sig * (1.0 + pre * (1.0 - sig)))).astype(bf16)
    backs = lax.dot_general(weights[...], dpre, CONTRACT_COLS, preferred_element_type=f32)
    grads = lax.dot_general(both, dpre, CONTRACT_ROWS, preferred_element_type=f32)
    bias_sum = jnp.sum(dpre.astype(f32), axis=0, keepdims=True)
    for p in range(PARTS):
        rows = []
        for t in range(3 * p, 3 * p + 3):
            r, h = t // WIDE, t % WIDE
            if t >= TILES:
                rows.append(jnp.zeros((8, BS), f32))
            elif t >= TILES - WIDE:
                rows.append(jnp.broadcast_to(bias_sum[:, h * BS:(h + 1) * BS], (8, BS)))
            else:
                rows.append(grads[r * 8:(r + 1) * 8, h * BS:(h + 1) * BS])
        grad_ref[p] = jnp.concatenate(rows, axis=0).astype(bf16)

    for b in range(BLOCKS_DEV):
        back = backs[F:, b * BS:(b + 1) * BS].astype(bf16)
        for k in range(0, K, 2):
            rhs = jnp.concatenate([tiles_ref[b, k], tiles_ref[b, k + 1]], axis=1)
            terms = jnp.dot(back, rhs, preferred_element_type=f32)
            one, two = place_ref[b, k], place_ref[b, k + 1]
            total[one] = total[one] + terms[:, :BS]
            total[two] = total[two] + terms[:, BS:]
    for j in range(BLOCKS_DEV):
        own = GROUP + BLOCKS_DEV * pos_ref[1] + j
        total[own] = total[own] + backs[:F, j * BS:(j + 1) * BS]
    for i in range(GROUP):
        away_ref[i] = total[beside_at + i].astype(bf16)
        kept_ref[0, i] = total[GROUP + i].astype(bf16)
        kept_ref[1, i] = total[across_at + i].astype(bf16)


def local_layer(pos, places, weights, bias, cotangent, tiles, mine, beside, across):
    return pl.pallas_call(
        layer_kernel,
        out_shape=(
            jax.ShapeDtypeStruct((ROWS, HID), bf16),
            jax.ShapeDtypeStruct((PARTS, PART, BS), bf16),
            jax.ShapeDtypeStruct((2, GROUP, F, BS), bf16),
            jax.ShapeDtypeStruct((GROUP, F, BS), bf16),
        ),
        in_specs=[SMEM] * 2 + [VMEM] * 7,
        out_specs=(VMEM,) * 4,
        scratch_shapes=[
            pltpu.VMEM((WINDOW + 1, BS, F), bf16),
            pltpu.VMEM((ROWS, 2 * F), bf16),
            pltpu.VMEM((WINDOW + 1, F, BS), f32),
        ],
        compiler_params=params(28),
        cost_estimate=cost(4 * BLOCKS_DEV * K * BS**3, 8 * 2**20),
        name="local_layer",
    )(pos, places, weights, bias, cotangent, tiles, mine, beside, across)


def chunk_kernel(kept_ref, beside_ref, stay_ref, send_ref):
    member = index_along(REP)
    for dy, out_ref in enumerate((stay_ref, send_ref)):
        for dx in range(ALONG_X):
            first = jnp.bitwise_xor(member, dy * ALONG_X + dx) * BLOCKS_DEV
            for j in range(BLOCKS_DEV):
                own = kept_ref[0, first + j].astype(f32) + beside_ref[first + j].astype(f32)
                out_ref[dx * PIECE + j] = own.astype(bf16)
                out_ref[dx * PIECE + BLOCKS_DEV + j] = kept_ref[1, first + j]


def chunks_of(kept, beside):
    return pl.pallas_call(
        chunk_kernel,
        out_shape=(jax.ShapeDtypeStruct((GROUP, F, BS), bf16),) * 2,
        in_specs=[VMEM] * 2,
        out_specs=(VMEM,) * 2,
        compiler_params=params(8),
        cost_estimate=cost(GROUP * F * BS, 3 * 2**20),
        name="chunks",
    )(kept, beside)


def sum_y_kernel(stay_ref, got_ref, here_ref, *send_refs):
    for i in range(PIECE):
        here_ref[i] = stay_ref[i].astype(f32) + got_ref[i].astype(f32)
    for d, send_ref in enumerate(send_refs):
        for i in range(PIECE):
            at = (d + 1) * PIECE + i
            send_ref[i] = (stay_ref[at].astype(f32) + got_ref[at].astype(f32)).astype(bf16)


def sum_y(stay, got):
    piece = (PIECE, F, BS)
    return pl.pallas_call(
        sum_y_kernel,
        out_shape=(jax.ShapeDtypeStruct(piece, f32),) + (jax.ShapeDtypeStruct(piece, bf16),) * (ALONG_X - 1),
        in_specs=[VMEM] * 2,
        out_specs=(VMEM,) * ALONG_X,
        compiler_params=params(8),
        cost_estimate=cost(GROUP * F * BS, 2 * 2**20),
        name="sum_y",
    )(stay, got)


def sum_x_kernel(here_ref, *refs):
    got_refs, (own_ref, across_ref) = refs[:-2], refs[-2:]
    for i in range(PIECE):
        acc = here_ref[i]
        for got_ref in got_refs:
            acc = acc + got_ref[i].astype(f32)
        if i < BLOCKS_DEV:
            own_ref[i] = acc
        else:
            across_ref[i - BLOCKS_DEV] = acc.astype(bf16)


def sum_x(here, got):
    return pl.pallas_call(
        sum_x_kernel,
        out_shape=(
            jax.ShapeDtypeStruct((BLOCKS_DEV, F, BS), f32),
            jax.ShapeDtypeStruct((BLOCKS_DEV, F, BS), bf16),
        ),
        in_specs=[VMEM] * ALONG_X,
        out_specs=(VMEM,) * 2,
        compiler_params=params(8),
        cost_estimate=cost(PIECE * ALONG_X * F * BS, 2**20),
        name="sum_x",
    )(here, *got)


def final_kernel(own_ref, across_ref, out_ref):
    for j in range(BLOCKS_DEV):
        terms = own_ref[j] + across_ref[j].astype(f32)
        out_ref[pl.ds(j * BS, BS)] = terms.T.astype(bf16)


def final_sum(own, across):
    return pl.pallas_call(
        final_kernel,
        out_shape=jax.ShapeDtypeStruct((ROWS, F), bf16),
        in_specs=[VMEM] * 2,
        out_specs=VMEM,
        compiler_params=params(8),
        cost_estimate=cost(ROWS * F, 2**19),
        name="final_sum",
    )(own, across)


def spread_kernel(scale, count, got_ref, out_ref):
    total = got_ref[0].astype(f32)
    for i in range(1, got_ref.shape[0]):
        total = total + got_ref[i].astype(f32)
    total = (total * scale).astype(bf16)
    for i in range(count):
        out_ref[i] = total


def sum_and_spread(got, scale, count):
    return pl.pallas_call(
        functools.partial(spread_kernel, scale, count),
        out_shape=jax.ShapeDtypeStruct((count,) + got.shape[1:], bf16),
        in_specs=[VMEM],
        out_specs=VMEM,
        compiler_params=params(8),
        cost_estimate=cost(got.size, 8 * got.size),
        name="sum_and_spread",
    )(got)


def unpack_kernel(parts_ref, self_ref, neigh_ref, bias_ref):
    for p in range(PARTS):
        part = parts_ref[p].astype(f32)
        for n in range(3):
            t = 3 * p + n
            if t >= TILES:
                continue
            r, lanes = t // WIDE, pl.ds((t % WIDE) * BS, BS)
            tile = part[n * 8:(n + 1) * 8]
            if t >= TILES - WIDE:
                bias_ref[:, lanes] = tile[:1]
            elif r < F // 8:
                self_ref[pl.ds(r * 8, 8), lanes] = tile
            else:
                neigh_ref[pl.ds(r * 8 - F, 8), lanes] = tile


def unpack(parts):
    return pl.pallas_call(
        unpack_kernel,
        out_shape=(
            jax.ShapeDtypeStruct((F, HID), f32),
            jax.ShapeDtypeStruct((F, HID), f32),
            jax.ShapeDtypeStruct((1, HID), f32),
        ),
        in_specs=[VMEM],
        out_specs=(VMEM,) * 3,
        compiler_params=params(8),
        cost_estimate=cost(parts.size, 8 * parts.size),
        name="unpack",
    )(parts)


def swapped(value, pairs):
    return lax.ppermute(value, BLK, pairs)


def exchanged(value, axes):
    return lax.all_to_all(value, axes, 0, 0)


def gathered(value):
    return exchanged(jnp.broadcast_to(value[None], (REPS,) + value.shape), REP)


def shards(cycle, feats, tiles, cols, counts, w_self, w_neigh, bias, cotangent):
    position = lax.axis_index(BLK)
    pos = jnp.stack([position, lax.axis_index(REP)]).astype(jnp.int32)
    places = window_places(cols, counts, position, cycle)
    weights = jnp.concatenate([w_self, w_neigh], axis=0)
    inner = [(i, i ^ 1) for i in range(cycle)]
    outer = [(i, (((i + 1) ^ 1) - 1) % cycle) for i in range(cycle)]
    across_rows = swapped(feats, outer)
    mine = gathered(feats)
    across = gathered(across_rows)
    beside = swapped(mine, inner)
    hidden, grad, kept, away = local_layer(
        pos, places, weights, bias.reshape(1, HID), cotangent, tiles, mine, beside, across,
    )
    split = ("z", "core")
    layers = ("yh",) + REP
    grad = exchanged(grad, split)
    stay, to_y = chunks_of(kept, swapped(away, inner))
    from_y = lax.ppermute(to_y, "yl", [(0, 1), (1, 0)])
    from_y, grad = lax.optimization_barrier((from_y, grad))
    grad = exchanged(sum_and_spread(grad, 1.0, YH * REPS), layers)
    here, *to_x = sum_y(stay, from_y)
    from_x = []
    for d in (2, 1, 3):
        from_x.append(lax.ppermute(to_x[d - 1], "x", [(x, x ^ d) for x in range(ALONG_X)]))
    own, to_across = sum_x(here, from_x)
    to_across, grad = lax.optimization_barrier((to_across, grad))
    factor = 1.0 / math.sqrt(cycle * REPS * ROWS)
    grad = exchanged(sum_and_spread(grad, factor, PARTS), split)
    grad_feats = final_sum(own, swapped(to_across, outer))
    grad_self, grad_neigh, grad_bias = unpack(grad)
    return (hidden, grad_feats, grad_self, grad_neigh, grad_bias.reshape(HID))


def solution(mesh):
    cycle, reps = mesh.shape["blk"], mesh.shape["rep"]
    split = Mesh(
        mesh.devices.reshape(YH, cycle // YH // 2, 2, 2, reps // 2), EVERY
    )
    in_specs = (
        P(EVERY, None),
        P(EVERY, None, None, None),
        P(EVERY, None),
        P(EVERY),
        P(),
        P(),
        P(),
        P(EVERY, None),
    )
    out_specs = (P(EVERY, None), P(EVERY, None), P(), P(), P())
    return jax.shard_map(
        functools.partial(shards, cycle),
        mesh=split, in_specs=in_specs, out_specs=out_specs, check_vma=False,
    )
```

```python
import functools
import math

import jax
import jax.numpy as jnp
from jax import lax
from jax.experimental import pallas as pl
from jax.experimental.pallas import tpu as pltpu
from jax.sharding import Mesh, PartitionSpec as P

BS = 128
K = 48
F = 128
HID = 256
GROUP = 16
BLOCKS_DEV = 2
SPAN = 3
REPS = 8
ROWS = BLOCKS_DEV * BS
WINDOW = SPAN * GROUP
REP = ("yl", "x")
BLK = ("yh", "z", "core")
EVERY = BLK + REP
YH = 4
ALONG_X = 4
PIECE = 2 * BLOCKS_DEV
PARTS = 24
PART = 24
WIDE = HID // BS
TILES = (2 * F // 8 + 1) * WIDE
bf16 = jnp.bfloat16
f32 = jnp.float32
SMEM = pl.BlockSpec(memory_space=pltpu.SMEM)
VMEM = pl.BlockSpec(memory_space=pltpu.VMEM)
CONTRACT_COLS = (((1,), (1,)), ((), ()))
CONTRACT_ROWS = (((0,), (0,)), ((), ()))


def params(mib):
    return pltpu.CompilerParams(vmem_limit_bytes=mib * 2**20)


def cost(flops, bytes_accessed):
    return pl.CostEstimate(flops=flops, bytes_accessed=bytes_accessed, transcendentals=0)


def window_places(cols, counts, position, cycle):
    blocks = cycle * GROUP
    places = (cols - (position - 1) * GROUP + blocks) % blocks
    used = jnp.arange(K, dtype=jnp.int32)[None, :] < counts[:, None]
    return jnp.where(used, places, WINDOW)


def index_along(axes):
    index = 0
    for axis in axes:
        index = index * lax.axis_size(axis) + lax.axis_index(axis)
    return index


def layer_kernel(
    pos_ref, place_ref, weights, bias_ref, cot,
    tiles_ref, mine_ref, beside_ref, across_ref,
    hidden_ref, grad_ref, kept_ref, away_ref,
    window, dense, total,
):
    even = jnp.bitwise_and(pos_ref[0], 1) == 0
    beside_at = jnp.where(even, 2 * GROUP, 0)
    across_at = jnp.where(even, 0, 2 * GROUP)
    window[WINDOW] = jnp.zeros((BS, F), bf16)
    for i in range(GROUP):
        r, rows = i // BLOCKS_DEV, pl.ds((i % BLOCKS_DEV) * BS, BS)
        window[GROUP + i] = mine_ref[r, rows]
        window[beside_at + i] = beside_ref[r, rows]
        window[across_at + i] = across_ref[r, rows]
    for i in range(WINDOW):
        total[i] = jnp.zeros((F, BS), f32)
    for b in range(BLOCKS_DEV):
        acc = jnp.zeros((BS, F), f32)
        for k in range(0, K, 2):
            lhs = jnp.concatenate([tiles_ref[b, k], tiles_ref[b, k + 1]], axis=1)
            rhs = jnp.concatenate([window[place_ref[b, k]], window[place_ref[b, k + 1]]], axis=0)
            acc = acc + jnp.dot(lhs, rhs, preferred_element_type=f32)
        dense[pl.ds(b * BS, BS), F:] = acc.astype(bf16)
    dense[:, :F] = mine_ref[pos_ref[1]]
    both = dense[...]
    pre = jnp.dot(both, weights[...], preferred_element_type=f32) + bias_ref[...]
    sig = jax.nn.sigmoid(pre)
    hidden_ref[...] = (pre * sig).astype(bf16)
    dpre = (cot[...].astype(f32) * (sig * (1.0 + pre * (1.0 - sig)))).astype(bf16)
    backs = lax.dot_general(weights[...], dpre, CONTRACT_COLS, preferred_element_type=f32)
    grads = lax.dot_general(both, dpre, CONTRACT_ROWS, preferred_element_type=f32)
    bias_sum = jnp.sum(dpre.astype(f32), axis=0, keepdims=True)
    for p in range(PARTS):
        rows = []
        for t in range(3 * p, 3 * p + 3):
            r, h = t // WIDE, t % WIDE
            if t >= TILES:
                rows.append(jnp.zeros((8, BS), f32))
            elif t >= TILES - WIDE:
                rows.append(jnp.broadcast_to(bias_sum[:, h * BS:(h + 1) * BS], (8, BS)))
            else:
                rows.append(grads[r * 8:(r + 1) * 8, h * BS:(h + 1) * BS])
        grad_ref[p] = jnp.concatenate(rows, axis=0).astype(bf16)

    for b in range(BLOCKS_DEV):
        back = backs[F:, b * BS:(b + 1) * BS].astype(bf16)
        for k in range(0, K, 2):
            rhs = jnp.concatenate([tiles_ref[b, k], tiles_ref[b, k + 1]], axis=1)
            terms = jnp.dot(back, rhs, preferred_element_type=f32)
            one, two = place_ref[b, k], place_ref[b, k + 1]
            total[one] = total[one] + terms[:, :BS]
            total[two] = total[two] + terms[:, BS:]
    for j in range(BLOCKS_DEV):
        own = GROUP + BLOCKS_DEV * pos_ref[1] + j
        total[own] = total[own] + backs[:F, j * BS:(j + 1) * BS]
    for i in range(GROUP):
        away_ref[i] = total[beside_at + i].astype(bf16)
        kept_ref[0, i] = total[GROUP + i].astype(bf16)
        kept_ref[1, i] = total[across_at + i].astype(bf16)


def local_layer(pos, places, weights, bias, cotangent, tiles, mine, beside, across):
    return pl.pallas_call(
        layer_kernel,
        out_shape=(
            jax.ShapeDtypeStruct((ROWS, HID), bf16),
            jax.ShapeDtypeStruct((PARTS, PART, BS), bf16),
            jax.ShapeDtypeStruct((2, GROUP, F, BS), bf16),
            jax.ShapeDtypeStruct((GROUP, F, BS), bf16),
        ),
        in_specs=[SMEM] * 2 + [VMEM] * 7,
        out_specs=(VMEM,) * 4,
        scratch_shapes=[
            pltpu.VMEM((WINDOW + 1, BS, F), bf16),
            pltpu.VMEM((ROWS, 2 * F), bf16),
            pltpu.VMEM((WINDOW + 1, F, BS), f32),
        ],
        compiler_params=params(28),
        cost_estimate=cost(4 * BLOCKS_DEV * K * BS**3, 8 * 2**20),
        name="local_layer",
    )(pos, places, weights, bias, cotangent, tiles, mine, beside, across)


def chunk_kernel(kept_ref, beside_ref, stay_ref, send_ref):
    member = index_along(REP)
    for dy, out_ref in enumerate((stay_ref, send_ref)):
        for dx in range(ALONG_X):
            first = jnp.bitwise_xor(member, dy * ALONG_X + dx) * BLOCKS_DEV
            for j in range(BLOCKS_DEV):
                own = kept_ref[0, first + j].astype(f32) + beside_ref[first + j].astype(f32)
                out_ref[dx * PIECE + j] = own.astype(bf16)
                out_ref[dx * PIECE + BLOCKS_DEV + j] = kept_ref[1, first + j]


def chunks_of(kept, beside):
    return pl.pallas_call(
        chunk_kernel,
        out_shape=(jax.ShapeDtypeStruct((GROUP, F, BS), bf16),) * 2,
        in_specs=[VMEM] * 2,
        out_specs=(VMEM,) * 2,
        compiler_params=params(8),
        cost_estimate=cost(GROUP * F * BS, 3 * 2**20),
        name="chunks",
    )(kept, beside)


def sum_y_kernel(stay_ref, got_ref, here_ref, *send_refs):
    for i in range(PIECE):
        here_ref[i] = stay_ref[i].astype(f32) + got_ref[i].astype(f32)
    for d, send_ref in enumerate(send_refs):
        for i in range(PIECE):
            at = (d + 1) * PIECE + i
            send_ref[i] = (stay_ref[at].astype(f32) + got_ref[at].astype(f32)).astype(bf16)


def sum_y(stay, got):
    piece = (PIECE, F, BS)
    return pl.pallas_call(
        sum_y_kernel,
        out_shape=(jax.ShapeDtypeStruct(piece, f32),) + (jax.ShapeDtypeStruct(piece, bf16),) * (ALONG_X - 1),
        in_specs=[VMEM] * 2,
        out_specs=(VMEM,) * ALONG_X,
        compiler_params=params(8),
        cost_estimate=cost(GROUP * F * BS, 2 * 2**20),
        name="sum_y",
    )(stay, got)


def sum_x_kernel(here_ref, *refs):
    got_refs, (own_ref, across_ref) = refs[:-2], refs[-2:]
    for i in range(PIECE):
        acc = here_ref[i]
        for got_ref in got_refs:
            acc = acc + got_ref[i].astype(f32)
        if i < BLOCKS_DEV:
            own_ref[i] = acc
        else:
            across_ref[i - BLOCKS_DEV] = acc.astype(bf16)


def sum_x(here, got):
    return pl.pallas_call(
        sum_x_kernel,
        out_shape=(
            jax.ShapeDtypeStruct((BLOCKS_DEV, F, BS), f32),
            jax.ShapeDtypeStruct((BLOCKS_DEV, F, BS), bf16),
        ),
        in_specs=[VMEM] * ALONG_X,
        out_specs=(VMEM,) * 2,
        compiler_params=params(8),
        cost_estimate=cost(PIECE * ALONG_X * F * BS, 2**20),
        name="sum_x",
    )(here, *got)


def final_kernel(own_ref, across_ref, out_ref):
    for j in range(BLOCKS_DEV):
        terms = own_ref[j] + across_ref[j].astype(f32)
        out_ref[pl.ds(j * BS, BS)] = terms.T.astype(bf16)


def final_sum(own, across):
    return pl.pallas_call(
        final_kernel,
        out_shape=jax.ShapeDtypeStruct((ROWS, F), bf16),
        in_specs=[VMEM] * 2,
        out_specs=VMEM,
        compiler_params=params(8),
        cost_estimate=cost(ROWS * F, 2**19),
        name="final_sum",
    )(own, across)


def spread_kernel(scale, count, got_ref, out_ref):
    total = got_ref[0].astype(f32)
    for i in range(1, got_ref.shape[0]):
        total = total + got_ref[i].astype(f32)
    total = (total * scale).astype(bf16)
    for i in range(count):
        out_ref[i] = total


def sum_and_spread(got, scale, count):
    return pl.pallas_call(
        functools.partial(spread_kernel, scale, count),
        out_shape=jax.ShapeDtypeStruct((count,) + got.shape[1:], bf16),
        in_specs=[VMEM],
        out_specs=VMEM,
        compiler_params=params(8),
        cost_estimate=cost(got.size, 8 * got.size),
        name="sum_and_spread",
    )(got)


def unpack_kernel(parts_ref, self_ref, neigh_ref, bias_ref):
    for p in range(PARTS):
        part = parts_ref[p].astype(f32)
        for n in range(3):
            t = 3 * p + n
            if t >= TILES:
                continue
            r, lanes = t // WIDE, pl.ds((t % WIDE) * BS, BS)
            tile = part[n * 8:(n + 1) * 8]
            if t >= TILES - WIDE:
                bias_ref[:, lanes] = tile[:1]
            elif r < F // 8:
                self_ref[pl.ds(r * 8, 8), lanes] = tile
            else:
                neigh_ref[pl.ds(r * 8 - F, 8), lanes] = tile


def unpack(parts):
    return pl.pallas_call(
        unpack_kernel,
        out_shape=(
            jax.ShapeDtypeStruct((F, HID), f32),
            jax.ShapeDtypeStruct((F, HID), f32),
            jax.ShapeDtypeStruct((1, HID), f32),
        ),
        in_specs=[VMEM],
        out_specs=(VMEM,) * 3,
        compiler_params=params(8),
        cost_estimate=cost(parts.size, 8 * parts.size),
        name="unpack",
    )(parts)


def swapped(value, pairs):
    return lax.ppermute(value, BLK, pairs)


def exchanged(value, axes):
    return lax.all_to_all(value, axes, 0, 0)


def gathered(value):
    return exchanged(jnp.broadcast_to(value[None], (REPS,) + value.shape), REP)


def shards(cycle, feats, tiles, cols, counts, w_self, w_neigh, bias, cotangent):
    position = lax.axis_index(BLK)
    pos = jnp.stack([position, lax.axis_index(REP)]).astype(jnp.int32)
    places = window_places(cols, counts, position, cycle)
    weights = jnp.concatenate([w_self, w_neigh], axis=0)
    inner = [(i, i ^ 1) for i in range(cycle)]
    outer = [(i, (((i + 1) ^ 1) - 1) % cycle) for i in range(cycle)]
    across_rows = swapped(feats, outer)
    mine = gathered(feats)
    across = gathered(across_rows)
    beside = swapped(mine, inner)
    hidden, grad, kept, away = local_layer(
        pos, places, weights, bias.reshape(1, HID), cotangent, tiles, mine, beside, across,
    )
    split = ("z", "core")
    layers = ("yh",) + REP
    grad = exchanged(grad, split)
    stay, to_y = chunks_of(kept, swapped(away, inner))
    from_y = lax.ppermute(to_y, "yl", [(0, 1), (1, 0)])
    from_y, grad = lax.optimization_barrier((from_y, grad))
    grad = exchanged(sum_and_spread(grad, 1.0, YH * REPS), layers)
    here, *to_x = sum_y(stay, from_y)
    from_x = []
    for d in (2, 3, 1):
        from_x.append(lax.ppermute(to_x[d - 1], "x", [(x, x ^ d) for x in range(ALONG_X)]))
    own, to_across = sum_x(here, from_x)
    to_across, grad = lax.optimization_barrier((to_across, grad))
    factor = 1.0 / math.sqrt(cycle * REPS * ROWS)
    grad = exchanged(sum_and_spread(grad, factor, PARTS), split)
    grad_feats = final_sum(own, swapped(to_across, outer))
    grad_self, grad_neigh, grad_bias = unpack(grad)
    return (hidden, grad_feats, grad_self, grad_neigh, grad_bias.reshape(HID))


def solution(mesh):
    cycle, reps = mesh.shape["blk"], mesh.shape["rep"]
    split = Mesh(
        mesh.devices.reshape(YH, cycle // YH // 2, 2, 2, reps // 2), EVERY
    )
    in_specs = (
        P(EVERY, None),
        P(EVERY, None, None, None),
        P(EVERY, None),
        P(EVERY),
        P(),
        P(),
        P(),
        P(EVERY, None),
    )
    out_specs = (P(EVERY, None), P(EVERY, None), P(), P(), P())
    return jax.shard_map(
        functools.partial(shards, cycle),
        mesh=split, in_specs=in_specs, out_specs=out_specs, check_vma=False,
    )
```
